32 devices in a mesh: groups: 2 (over x), ctx: 8 (over z, y), head: 2 (over core).
Axes of the slice: x: 2, y: 2, z: 4, core: 2. Of those that a mesh axis runs over, the one named last changes fastest.
Arguments:
- features: bfloat16 [8192, 8192], P(('groups', 'ctx'), 'head'), parts along dimension 0, may hold values from -6 to 6
- output_switch: bfloat16 [8192, 8192], P(('groups', 'ctx'), 'head'), parts along dimension 0, may hold values from -6 to 6
- input_proj: bfloat16 [8192, 512], P(('groups', 'ctx'), 'head'), parts along dimension 0, may hold values from -1.796875 to 1.796875
- output_proj: bfloat16 [8192, 512], P(('groups', 'ctx'), 'head'), parts along dimension 0, may hold values from -1.796875 to 1.796875
- step_codes: int32 [8192, 128], P(('groups', 'ctx'), 'head'), parts along dimension 0, may hold values from 1 to 12288
- head_rate: float32 [128], P('head'), may hold values from 0 to 12
- conv_weight: bfloat16 [4, 8192], P(None, 'head'), may hold values from -3 to 3
- conv_bias: bfloat16 [8192], P('head'), may hold values from -3 to 3
- bypass_factor: float32 [128], P('head'), may hold values from 2 to 32
- norm_gain: float32 [8192], P('head'), may hold values from 0.5 to 1.5
Outputs:
- ssm_output: bfloat16 [8192, 8192], P(('groups', 'ctx'), 'head'), parts along dimension 0
The draws below stay inside these ranges and needn't reach their ends.
There are 2 independent parts, one for each index of `groups`. The reference program is written for one: setup_inputs(seed, part) draws one part's arguments, and reference() takes and returns one part's arrays. A program takes and returns all parts, laid end to end along the dimension named above; an argument that names none is the same for every part. Nothing has to cross between parts.
All inputs are finite; a program needn't handle non-finite values.
Results may differ from the reference program's by a relative error of at most 0.0063.
Values may be sent and summed in bfloat16 or wider, within the bound.
No kernel may reach another device: no remote copies, remote signals or barrier semaphores. Data moves between devices by JAX's collectives and lax.ppermute only.
A program may use at most 128 MiB of HBM per device.

```python
import math
import jax
import jax.numpy as jnp
from jax import lax

HEADS = 128
HEAD_DIM = 64
NSTATE = 128
GROUPS = 4
KERNEL = 4
BLOCK = 512
PIECE_LENGTH = 4096


def draw_step_codes(key, part):
    key = jax.random.fold_in(key, 11)
    key_base, key_factor, key_spots = jax.random.split(key, 3)
    nblocks = PIECE_LENGTH // BLOCK
    base_codes = jax.random.randint(key_base, (nblocks, BLOCK, HEADS), 1, 4)
    factors = jax.random.randint(key_factor, (nblocks, 1, HEADS), 1, 3)
    quantized_labels = (base_codes * factors).reshape(PIECE_LENGTH, HEADS)
    storage_targets = jax.random.randint(key_spots, (3,), 0, PIECE_LENGTH)
    sequence_places = jnp.arange(PIECE_LENGTH)
    symbol_groupings = jnp.any(sequence_places[:, None] == storage_targets[None, :], axis=1)
    quantized_labels = jnp.where(symbol_groupings[:, None], 3 * PIECE_LENGTH, quantized_labels)
    return quantized_labels.astype(jnp.int32)


def draw_head_rate(key, part):
    key = jax.random.fold_in(key, 23)
    key_fast, key_slow, key_quick = jax.random.split(key, 3)
    fast_share = 0.5
    chooser = jax.random.uniform(key_fast, (HEADS,), jnp.float32)
    slow_rate = jax.random.uniform(key_slow, (HEADS,), jnp.float32, 0.25, 0.5) * 1024.0 / (3.0 * PIECE_LENGTH)
    fast_rate = 1024.0 / 3.0 / jax.random.uniform(key_quick, (HEADS,), jnp.float32, 30.0, 50.0)
    return jnp.where(chooser < fast_share, fast_rate, slow_rate).astype(jnp.float32)


def shard_levels(key, shape, shards, smallest, top_value):
    def one(position, parts):
        steps = jax.random.uniform(jax.random.fold_in(jax.random.fold_in(key, 6), position), (parts,), jnp.float32, smallest / len(shards), top_value / len(shards))
        return jnp.repeat(jnp.exp(steps), shape[position] // parts).reshape((-1,) + (1,) * (len(shape) - position - 1))

    gain = one(*shards[0])
    for cut in shards[1:]:
        gain = gain * one(*cut)
    return gain


def gaussian(stream_key, shape, scale, reach, shards=(), held_as=jnp.bfloat16):
    level = shard_levels(stream_key, shape, shards, -0.22, 0.18) if shards else 1.0
    array = jax.random.normal(stream_key, shape, jnp.float32) * scale * level
    return jnp.minimum(jnp.maximum(array, -reach), reach).astype(held_as)


def setup_inputs(seed: int = 0, part: int = 0) -> dict:
    seeds = jax.random.split(jax.random.key(seed), 11)
    part_keys = jax.random.split(jax.random.fold_in(seeds[10], part), 11)
    features = gaussian(part_keys[0], (PIECE_LENGTH, HEADS * HEAD_DIM), 1.0, 6.0, ((0, 8), (1, 2)))
    output_switch = gaussian(part_keys[1], (PIECE_LENGTH, HEADS * HEAD_DIM), 1.0, 6.0, ((0, 8), (1, 2)))
    input_proj = gaussian(part_keys[2], (PIECE_LENGTH, GROUPS * NSTATE), 0.3, 1.796875, ((0, 8), (1, 2)))
    output_proj = gaussian(part_keys[3], (PIECE_LENGTH, GROUPS * NSTATE), 0.3, 1.796875, ((0, 8), (1, 2)))
    step_codes = draw_step_codes(jax.random.fold_in(jax.random.fold_in(seeds[10], part), 71), part)
    head_rate = draw_head_rate(jax.random.fold_in(seeds[10], 71), part)
    conv_weight = gaussian(seeds[6], (KERNEL, HEADS * HEAD_DIM), KERNEL ** -0.5, 3.0, ((1, 2),))
    conv_bias = gaussian(seeds[7], (HEADS * HEAD_DIM,), 0.5, 3.0, ((0, 2),))
    bypass_factor = jnp.clip(jnp.exp(math.log(32.0) - 2.7725887 * jax.random.uniform(seeds[8], (HEADS,), jnp.float32) ** shard_levels(seeds[8], (HEADS,), ((0, 2),), -0.2, 0.2)), 2.0, 32.0)
    norm_gain = jnp.clip(1.0 + 0.1 * jax.random.normal(seeds[9], (HEADS * HEAD_DIM,), jnp.float32), 0.5, 1.5)
    return dict(features=features, output_switch=output_switch, input_proj=input_proj, output_proj=output_proj, step_codes=step_codes, head_rate=head_rate, conv_weight=conv_weight, conv_bias=conv_bias, bypass_factor=bypass_factor, norm_gain=norm_gain)


highest = lax.Precision.HIGHEST
code_unit = 1024.0

def rounded(values):
    return lax.optimization_barrier(values.astype(jnp.bfloat16)).astype(jnp.float32)

def conv_filter(features, conv_weight, conv_bias):
    length = features.shape[0]
    padded = jnp.concatenate([jnp.zeros((KERNEL - 1, features.shape[1]), jnp.bfloat16), features], axis=0)
    summed_values = jnp.zeros(features.shape, jnp.float32) + conv_bias.astype(jnp.float32)[None, :]
    for start_offset in range(KERNEL):
        summed_values = summed_values + conv_weight[start_offset].astype(jnp.float32)[None, :] * padded[start_offset:start_offset + length].astype(jnp.float32)
    return (summed_values * jax.nn.sigmoid(summed_values)).astype(jnp.bfloat16)

def reference(features, output_switch, input_proj, output_proj, step_codes, head_rate, conv_weight, conv_bias, bypass_factor, norm_gain):
    per_group = HEADS // GROUPS
    nblocks = PIECE_LENGTH // BLOCK
    filtered = conv_filter(features, conv_weight, conv_bias)
    log_decay = -(head_rate[None, :] * (step_codes.astype(jnp.float32) / code_unit))
    cumulative = jnp.cumsum(log_decay.reshape(nblocks, BLOCK, HEADS), axis=1)
    block_total = cumulative[:, -1, :]
    filt_blocks = filtered.reshape(nblocks, BLOCK, GROUPS, per_group, HEAD_DIM).astype(jnp.float32)
    write_blocks = input_proj.reshape(nblocks, BLOCK, GROUPS, NSTATE).astype(jnp.float32)
    read_blocks = output_proj.reshape(nblocks, BLOCK, GROUPS, NSTATE).astype(jnp.float32)
    gate_blocks = output_switch.reshape(nblocks, BLOCK, HEADS, HEAD_DIM).astype(jnp.float32)

    def block_state(operands):
        filt, writes, cumul = operands
        weights_end = jnp.exp(cumul[-1:, :] - cumul).reshape(BLOCK, GROUPS, per_group)
        weighted = rounded(weights_end[..., None] * filt)
        summed_values = jnp.einsum('jgkp,jgn->gkpn', weighted, writes, precision=highest)
        return summed_values.reshape(HEADS, HEAD_DIM, NSTATE)
    states = lax.map(block_state, (filt_blocks, write_blocks, cumulative))

    def advance(running, operands):
        state_now, total_now = operands
        return (jnp.exp(total_now)[:, None, None] * running + state_now, running)
    _, entering = lax.scan(advance, jnp.zeros((HEADS, HEAD_DIM, NSTATE), jnp.float32), (states, block_total))
    causal = jnp.arange(BLOCK)[:, None] >= jnp.arange(BLOCK)[None, :]

    def block_output(operands):
        filt, writes, reads, cumul, entry, gates = operands
        scores = jnp.einsum('tgn,jgn->gtj', reads, writes, precision=highest)
        cumul_heads = cumul.T
        spread = cumul_heads[:, :, None] - cumul_heads[:, None, :]
        decays = jnp.where(causal[None], jnp.exp(jnp.where(causal[None], spread, 0.0)), 0.0)
        mixing = rounded(decays.reshape(GROUPS, per_group, BLOCK, BLOCK) * scores[:, None])
        inside = jnp.einsum('gktj,jgkp->tgkp', mixing, filt, precision=highest)
        carried_state = rounded(entry).reshape(GROUPS, per_group, HEAD_DIM, NSTATE)
        carried = jnp.einsum('tgn,gkpn->tgkp', reads, carried_state, precision=highest)
        growth = jnp.exp(cumul).reshape(BLOCK, GROUPS, per_group)[..., None]
        output_pre = inside + growth * carried + bypass_factor.reshape(GROUPS, per_group)[None, :, :, None] * filt
        output_pre = output_pre.reshape(BLOCK, HEADS, HEAD_DIM)
        gated = output_pre * gates * jax.nn.sigmoid(gates)
        meansq = lax.optimization_barrier(jnp.mean(gated * gated, axis=-1, keepdims=True))
        normed = gated * lax.rsqrt(meansq + 1e-05) * norm_gain.reshape(HEADS, HEAD_DIM)
        return normed.astype(jnp.bfloat16).reshape(BLOCK, HEADS * HEAD_DIM)
    outputs = lax.map(block_output, (filt_blocks, write_blocks, read_blocks, cumulative, entering, gate_blocks))
    return outputs.reshape(PIECE_LENGTH, HEADS * HEAD_DIM)
```

```python
import functools
import math

import jax
import jax.numpy as jnp
from jax import lax
from jax.experimental import pallas as pl
from jax.experimental.pallas import tpu as pltpu
from jax.sharding import PartitionSpec as P

NSTATE = 128
KERNEL = 4
BLOCK = 512
HEAD_DIM = 64
SUB = 128
NSUB = BLOCK // SUB
CHUNKS = 4
LANES = 512
ILANES = 1024
TAIL = 8

f32 = jnp.float32
bf16 = jnp.bfloat16
LOG2E = math.log2(math.e)
VMEM_LIMIT = 40 * 1024 * 1024


def iota(shape, axis):
    return lax.broadcasted_iota(jnp.int32, shape, axis)


def dot(a, b):
    return jnp.dot(a, b, preferred_element_type=f32)


def half_tanh_gate(values):
    return values * (0.5 * jnp.tanh(0.5 * values) + 0.5)


def spread_matrix(first_head, heads, lanes):
    row = iota((4 * heads, lanes), 0)
    lane = iota((4 * heads, lanes), 1)
    hit = (row % heads) == first_head + lane // HEAD_DIM
    part = row // heads
    scale = jnp.where(part == 0, 65536.0, jnp.where(part == 1, 256.0, jnp.where(part == 2, 1.0, 0.0)))
    return jnp.where(hit, scale, 0.0).astype(bf16)


def prep_kernel(codes_ref, heads_ref, b_ref, c_ref, pieces_ref, left_ref, right_ref, scores_ref, bt_ref, rows_ref):
    tokens, heads = codes_ref.shape
    width = rows_ref.shape[1]
    groups = b_ref.shape[1] // NSTATE
    codes = codes_ref[...]
    split = jnp.concatenate([codes >> 8, codes & 255], axis=1).astype(f32).astype(bf16)
    causal = iota((SUB, SUB), 0) >= iota((SUB, SUB), 1)
    lower = jnp.where(causal, 1.0, 0.0).astype(bf16)
    sums = jnp.concatenate([dot(lower, split[s * SUB : (s + 1) * SUB]) for s in range(NSUB)], axis=0)
    whole = sums[:, :heads].astype(jnp.int32) * 256 + sums[:, heads:].astype(jnp.int32)
    first, second, third = whole >> 16, (whole >> 8) & 255, whole & 255
    pieces = jnp.concatenate([first, second, third, jnp.zeros_like(first)], axis=1).astype(f32).astype(bf16)
    pieces_ref[...] = pieces
    row = iota((4 * heads, 8 * heads), 0)
    col = iota((4 * heads, 8 * heads), 1)
    kind = col % 8
    same = ((row % heads) == col // 8) & (row < 3 * heads)
    to_left = jnp.where(same & (row // heads == kind), 1.0, 0.0).astype(bf16)
    col_kind = iota((tokens, 8 * heads), 1) % 8
    left = dot(pieces, to_left) + jnp.where((col_kind >= 3) & (col_kind < 6), 1.0, 0.0)
    left_ref[...] = left.astype(bf16)
    scale = jnp.where(kind == 3, -65536.0, jnp.where(kind == 4, -256.0, -1.0))
    to_right = jnp.where(same & (row // heads == kind - 3), scale, 0.0).astype(bf16)
    fixed = jnp.where(col_kind == 0, 65536.0, jnp.where(col_kind == 1, 256.0, jnp.where(col_kind == 2, 1.0, 0.0)))
    right = dot(pieces, to_right) + fixed
    right_ref[...] = right.T.astype(bf16)
    for g in range(groups):
        cols = slice(g * NSTATE, (g + 1) * NSTATE)
        bt = b_ref[:, cols].astype(f32).T.astype(bf16)
        bt_ref[cols, :] = bt
        for s in range(NSUB):
            rows = slice(s * SUB, (s + 1) * SUB)
            scores = dot(c_ref[rows, cols], bt[:, rows])
            scores_ref[g, rows, :] = jnp.where(causal, scores, 0.0)
    spread = jnp.where(iota((heads, width), 0) == iota((heads, width), 1) // HEAD_DIM, 1.0, 0.0)
    totals = jnp.concatenate(
        [whole[(s + 1) * SUB - 1 : (s + 1) * SUB] for s in range(NSUB)], axis=0
    ).astype(f32)
    small = jnp.concatenate([heads_ref[...], totals, jnp.zeros_like(totals)], axis=0)
    wide = jnp.dot(small, spread, precision=lax.Precision.HIGHEST, preferred_element_type=f32)
    rate = wide[0:1] * (-LOG2E / 1024.0)
    base = jnp.zeros_like(rate)
    rows_ref[0:1, :] = rate
    rows_ref[1:2, :] = wide[1:2]
    for s in range(NSUB):
        total = wide[8 + s : 9 + s]
        rows_ref[2 + s : 3 + s, :] = jnp.exp2(rate * total)
        rows_ref[8 + s : 9 + s, :] = jnp.exp2(rate * base)
        base = base + total
    rows_ref[6:7, :] = jnp.exp2(rate * base)
    rows_ref[7:8, :] = jnp.zeros_like(rate)
    rows_ref[12:16, :] = jnp.zeros((4, width), f32)


def state_kernel(first_block, x_ref, tail_ref, w_ref, bias_ref, pieces_ref, bt_ref, rows_ref, f_ref, local_ref, state_ref):
    lanes = x_ref.shape[1]
    heads = pieces_ref.shape[1] // 4
    first_head = (first_block + pl.program_id(0)) * (lanes // HEAD_DIM)
    padded = jnp.concatenate([tail_ref[...].astype(f32), x_ref[...].astype(f32)], axis=0)
    weights = w_ref[...].astype(f32)
    summed = bias_ref[...].astype(f32) + weights[KERNEL - 1 : KERNEL] * padded[TAIL:]
    for back in range(1, KERNEL):
        moved = pltpu.roll(padded, back, 0)[TAIL:]
        summed = summed + weights[KERNEL - 1 - back : KERNEL - back] * moved
    filtered = half_tanh_gate(summed).astype(bf16)
    f_ref[...] = filtered
    spread = spread_matrix(first_head, heads, lanes)
    rate = rows_ref[0:1, :]
    running = None
    for s in range(NSUB):
        rows = slice(s * SUB, (s + 1) * SUB)
        wide = dot(pieces_ref[rows, :], spread)
        weight = jnp.exp2(rate * (wide[SUB - 1 : SUB] - wide))
        weighted = (weight * filtered[rows].astype(f32)).astype(bf16)
        part = dot(bt_ref[:, rows], weighted)
        running = part if s == 0 else rows_ref[2 + s : 3 + s, :] * running + part
        if s < NSUB - 1:
            local_ref[s] = running.astype(bf16)
    state_ref[...] = running.astype(bf16)


def inside_kernel(first_block, per_block, f_ref, local_ref, z_ref, c_ref, pieces_ref, left_ref, right_ref, scores_ref, rows_ref, rate_ref, p_ref, g_ref, wall):
    lanes = f_ref.shape[1]
    here = lanes // HEAD_DIM
    heads = pieces_ref.shape[1] // 4
    first_head = (first_block + pl.program_id(0)) * here
    spread = spread_matrix(first_head, heads, lanes)
    rate = rows_ref[0:1, :]
    bypass = rows_ref[1:2, :]
    wall[...] = jnp.zeros_like(wall)
    upper = iota((16, SUB), 0) < 8
    first_lanes = iota((SUB, 128), 1) < HEAD_DIM
    for s in range(NSUB):
        rows = slice(s * SUB, (s + 1) * SUB)
        for q in range(here // 2):
            tile = right_ref[16 * q : 16 * q + 16, rows].astype(f32)
            wall[16 * q : 16 * q + 16, 2 * q * SUB : (2 * q + 1) * SUB] = jnp.where(upper, tile, 0.0).astype(bf16)
            wall[16 * q : 16 * q + 16, (2 * q + 1) * SUB : (2 * q + 2) * SUB] = jnp.where(upper, 0.0, tile).astype(bf16)
        scores = scores_ref[0, rows, :]
        left = left_ref[rows, :]
        wide = dot(pieces_ref[rows, :], spread)
        growth = jnp.exp2(rate * wide)
        filtered = f_ref[rows, :].astype(f32)
        gate = half_tanh_gate(z_ref[rows, :].astype(f32))
        g_ref[rows, :] = (gate * growth * rows_ref[8 + s : 9 + s, :]).astype(bf16)
        total = bypass * filtered
        if s > 0:
            total = total + growth * dot(c_ref[rows, :], local_ref[s - 1])
        for q in range(here // 2):
            spans = dot(left, wall[:, 2 * q * SUB : (2 * q + 2) * SUB])
            mixing = []
            for k in range(2):
                scale = rate_ref[first_head + 2 * q + k] * (-LOG2E / 1024.0)
                decays = jnp.exp2(jnp.maximum(spans[:, k * SUB : (k + 1) * SUB], 0.0) * scale)
                mixing.append((decays * scores).astype(bf16))
            mine = filtered[:, 128 * q : 128 * q + 128]
            stacked = jnp.concatenate(
                [jnp.where(first_lanes, mine, 0.0), jnp.where(first_lanes, 0.0, mine)], axis=0
            ).astype(bf16)
            inside = dot(jnp.concatenate(mixing, axis=1), stacked)
            cols = slice(128 * q, 128 * q + 128)
            p_ref[rows, cols] = ((total[:, cols] + inside) * gate[:, cols]).astype(bf16)


def final_kernel(p_ref, g_ref, e_ref, c_ref, gain_ref, *rest):
    out_ref = rest[-1]
    lanes = p_ref.shape[1]
    same = iota((256, 256), 0) // HEAD_DIM == iota((256, 256), 1) // HEAD_DIM
    mean = jnp.where(same, 1.0 / HEAD_DIM, 0.0).astype(bf16)
    for q in range(lanes // 256):
        cols = slice(256 * q, 256 * q + 256)
        carried = dot(c_ref[...], e_ref[:, cols])
        gated = p_ref[:, cols].astype(f32) + carried * g_ref[:, cols].astype(f32)
        meansq = dot((gated * gated).astype(bf16), mean)
        out_ref[:, cols] = (gated * lax.rsqrt(meansq + 1e-05) * gain_ref[:, cols]).astype(bf16)


def params():
    return pltpu.CompilerParams(vmem_limit_bytes=VMEM_LIMIT)


def full(shape):
    return pl.BlockSpec(shape, lambda i: (0,) * len(shape))


def per_device(
    features,
    output_switch,
    input_proj,
    output_proj,
    step_codes,
    head_rate,
    conv_weight,
    conv_bias,
    bypass_factor,
    norm_gain,
):
    tokens, width = features.shape
    heads = head_rate.shape[0]
    groups = input_proj.shape[1] // NSTATE
    assert tokens == BLOCK and width == heads * HEAD_DIM
    runs = lax.axis_size("ctx")
    pairs = runs // 2
    odd = lax.axis_index("ctx") % 2 == 1
    swap = [(i, i ^ 1) for i in range(runs)]

    tail = lax.ppermute(features[tokens - TAIL :], "ctx", [(i, i + 1) for i in range(runs - 1)])

    def shape(dims, dtype):
        return jax.ShapeDtypeStruct(dims, dtype)

    small = jnp.concatenate([head_rate[None], bypass_factor[None], jnp.zeros((6, heads), f32)], axis=0)
    pieces, left, right, scores, bt, rows = pl.pallas_call(
        prep_kernel,
        out_shape=(
            shape((tokens, 4 * heads), bf16),
            shape((tokens, 8 * heads), bf16),
            shape((8 * heads, tokens), bf16),
            shape((groups, tokens, SUB), f32),
            shape((groups * NSTATE, tokens), bf16),
            shape((16, width), f32),
        ),
        compiler_params=params(),
        cost_estimate=pl.CostEstimate(flops=1 << 28, bytes_accessed=1 << 22, transcendentals=0),
    )(step_codes, small, input_proj, output_proj)

    decay_own = rows[6:7]
    decay_other = lax.ppermute(decay_own, "ctx", swap)
    decay_even = jnp.where(odd, decay_other, decay_own)
    decay_odd = jnp.where(odd, decay_own, decay_other)
    decay_pair = decay_even * decay_odd

    bias = conv_bias[None]
    gain = norm_gain[None]
    share = width // CHUNKS
    group_width = width // groups
    half = NSTATE // 2

    def conv_states(c):
        steps = share // LANES
        first = c * steps
        column = lambda i: (0, first + i)
        return pl.pallas_call(
            functools.partial(state_kernel, first),
            grid=(steps,),
            in_specs=[
                pl.BlockSpec((tokens, LANES), column),
                pl.BlockSpec((TAIL, LANES), column),
                pl.BlockSpec((KERNEL, LANES), column),
                pl.BlockSpec((1, LANES), column),
                full((tokens, 4 * heads)),
                pl.BlockSpec((NSTATE, tokens), lambda i: ((first + i) * LANES // group_width, 0)),
                pl.BlockSpec((16, LANES), column),
            ],
            out_specs=[
                pl.BlockSpec((tokens, LANES), lambda i: (0, i)),
                pl.BlockSpec((NSUB - 1, NSTATE, LANES), lambda i: (0, 0, i)),
                pl.BlockSpec((NSTATE, LANES), lambda i: (0, i)),
            ],
            out_shape=(
                shape((tokens, share), bf16),
                shape((NSUB - 1, NSTATE, share), bf16),
                shape((NSTATE, share), bf16),
            ),
            compiler_params=params(),
            cost_estimate=pl.CostEstimate(flops=1 << 30, bytes_accessed=3 << 20, transcendentals=0),
        )(features, tail, conv_weight, bias, pieces, bt, rows)

    def inside(c, filtered, local):
        steps = share // ILANES
        first = c * steps
        block_heads = ILANES // HEAD_DIM
        column = lambda i: (0, first + i)
        return pl.pallas_call(
            functools.partial(inside_kernel, first, block_heads),
            grid=(steps,),
            in_specs=[
                pl.BlockSpec((tokens, ILANES), lambda i: (0, i)),
                pl.BlockSpec((NSUB - 1, NSTATE, ILANES), lambda i: (0, 0, i)),
                pl.BlockSpec((tokens, ILANES), column),
                pl.BlockSpec((tokens, NSTATE), lambda i: (0, (first + i) * ILANES // group_width)),
                full((tokens, 4 * heads)),
                pl.BlockSpec((tokens, 8 * block_heads), column),
                pl.BlockSpec((8 * block_heads, tokens), lambda i: (first + i, 0)),
                pl.BlockSpec((1, tokens, SUB), lambda i: ((first + i) * ILANES // group_width, 0, 0)),
                pl.BlockSpec((16, ILANES), column),
                pl.BlockSpec(memory_space=pltpu.SMEM),
            ],
            out_specs=[
                pl.BlockSpec((tokens, ILANES), lambda i: (0, i)),
                pl.BlockSpec((tokens, ILANES), lambda i: (0, i)),
            ],
            out_shape=(shape((tokens, share), bf16), shape((tokens, share), bf16)),
            scratch_shapes=[pltpu.VMEM((8 * block_heads, block_heads * SUB), bf16)],
            compiler_params=params(),
            cost_estimate=pl.CostEstimate(flops=3 << 30, bytes_accessed=5 << 20, transcendentals=0),
        )(filtered, local, output_switch, output_proj, pieces, left, right, scores, rows, head_rate)

    def final(c, out, kept, growth, entering):
        steps = share // LANES
        first = c * steps
        column = lambda i: (0, first + i)
        mine = lambda i: (0, i)
        operands = [kept, growth, entering, output_proj, gain]
        in_specs = [
            pl.BlockSpec((tokens, LANES), mine),
            pl.BlockSpec((tokens, LANES), mine),
            pl.BlockSpec((NSTATE, LANES), mine),
            pl.BlockSpec((tokens, NSTATE), lambda i: (0, (first + i) * LANES // group_width)),
            pl.BlockSpec((1, LANES), column),
        ]
        aliases = {}
        if out is not None:
            aliases = {len(operands): 0}
            operands.append(out)
            in_specs.append(pl.BlockSpec(memory_space=pl.ANY))
        return pl.pallas_call(
            final_kernel,
            grid=(steps,),
            in_specs=in_specs,
            out_specs=pl.BlockSpec((tokens, LANES), column),
            out_shape=shape((tokens, width), bf16),
            input_output_aliases=aliases,
            compiler_params=params(),
            cost_estimate=pl.CostEstimate(flops=1 << 29, bytes_accessed=3 << 20, transcendentals=0),
        )(*operands)

    def carry(c, state):
        cols = slice(c * share, (c + 1) * share)
        even, pair = decay_even[:, cols], decay_pair[:, cols]
        later = decay_odd[:, cols]
        low, high = state[:half], state[half:]
        own = jnp.where(odd, high, low)
        got = lax.ppermute(jnp.where(odd, low, high), "ctx", swap)
        before = jnp.where(odd, got, own).astype(f32)
        after = jnp.where(odd, own, got).astype(f32)
        both = later * before + after
        entering = jnp.zeros_like(both)
        for step in range(pairs - 1):
            sent = (pair * entering + both).astype(bf16)
            route = [(2 * step + k, 2 * step + 2 + k) for k in range(2)]
            entering = entering + lax.ppermute(sent, "ctx", route).astype(f32)
        between = (even * entering + before).astype(bf16)
        entering = entering.astype(bf16)
        mine = jnp.where(odd, between, entering)
        other = lax.ppermute(jnp.where(odd, entering, between), "ctx", swap)
        return jnp.concatenate([jnp.where(odd, other, mine), jnp.where(odd, mine, other)], axis=0)

    parts = [conv_states(c) for c in range(CHUNKS)]
    insides = [inside(c, parts[c][0], parts[c][1]) for c in range(CHUNKS)]
    entering = [carry(c, parts[c][2]) for c in range(CHUNKS)]
    out = None
    for c in range(CHUNKS):
        out = final(c, out, insides[c][0], insides[c][1], entering[c])
    return out


def solution(mesh):
    placed = (
        P(("groups", "ctx"), "head"),
        P(("groups", "ctx"), "head"),
        P(("groups", "ctx"), "head"),
        P(("groups", "ctx"), "head"),
        P(("groups", "ctx"), "head"),
        P("head"),
        P(None, "head"),
        P("head"),
        P("head"),
        P("head"),
    )
    return jax.shard_map(
        per_device,
        mesh=mesh,
        in_specs=placed,
        out_specs=P(("groups", "ctx"), "head"),
        check_vma=False,
    )
```

```python
import functools
import math

import jax
import jax.numpy as jnp
from jax import lax
from jax.experimental import pallas as pl
from jax.experimental.pallas import tpu as pltpu
from jax.sharding import PartitionSpec as P

NSTATE = 128
KERNEL = 4
BLOCK = 512
HEAD_DIM = 64
SUB = 128
NSUB = BLOCK // SUB
WIDTHS = (2048, 2048)
HEAD_SHIFT = 6
LANES = 512
ILANES = 512
FLANES = 1024
TILE = 256
IWIDTH = 1024
TAIL = 8

f32 = jnp.float32
bf16 = jnp.bfloat16
LOG2E = math.log2(math.e)
MIB = 1024 * 1024
PREP_LIMIT, STATE_LIMIT, INSIDE_LIMIT, FINAL_LIMIT = 16, 16, 16, 16
PREP_BYTES, STATE_BYTES, INSIDE_BYTES, FINAL_BYTES = 1, 1, 1, 1


def iota(shape, axis):
    return lax.broadcasted_iota(jnp.int32, shape, axis)


def dot(a, b):
    return jnp.dot(a, b, preferred_element_type=f32)


def silu_of_twice(values):
    return values + values * jnp.tanh(values)


def bits(size):
    return size.bit_length() - 1


def prep_kernel(
    codes_hbm, rate_hbm, bypass_hbm, b_hbm, w_hbm, bias_hbm,
    pieces_ref, spread_ref, bt_ref, rows_ref, taps_ref, decay_ref, odd_ref,
    codes_ref, rate_ref, bypass_ref, b_ref, w_ref, bias_ref, sems,
):
    pairs = (
        (codes_hbm, codes_ref), (rate_hbm, rate_ref), (bypass_hbm, bypass_ref), (b_hbm, b_ref),
        (w_hbm, w_ref), (bias_hbm, bias_ref),
    )
    copies = [pltpu.make_async_copy(a, b, sems.at[k]) for k, (a, b) in enumerate(pairs)]
    for copy in copies:
        copy.start()
    heads, tokens = codes_ref.shape
    width = rows_ref.shape[1]
    groups = b_ref.shape[1] // NSTATE
    per_group = heads // groups
    group_width = width // groups
    causal = iota((SUB, SUB), 0) >= iota((SUB, SUB), 1)
    lower = jnp.where(causal, 1.0, 0.0).astype(bf16)
    row = iota((4 * per_group, group_width), 0)
    part = row >> bits(per_group)
    hit = (row & (per_group - 1)) == (iota((4 * per_group, group_width), 1) >> HEAD_SHIFT)
    scale = jnp.where(part == 0, 65536.0, jnp.where(part == 1, 256.0, jnp.where(part == 2, 1.0, 0.0)))
    spread_ref[...] = jnp.where(hit, scale, 0.0).astype(bf16)
    odd = (lax.axis_index("ctx") & 1) == 1
    odd_ref[...] = jnp.where(odd, jnp.ones(odd_ref.shape, f32), 0.0)
    spread = jnp.where(iota((heads, width), 0) == (iota((heads, width), 1) >> HEAD_SHIFT), 1.0, 0.0)
    for copy in copies:
        copy.wait()
    codes = codes_ref[...].T
    split = jnp.concatenate([codes >> 8, codes & 255], axis=1).astype(f32).astype(bf16)
    sums = jnp.concatenate([dot(lower, split[s * SUB : (s + 1) * SUB]) for s in range(NSUB)], axis=0)
    whole = sums[:, :heads].astype(jnp.int32) * 256 + sums[:, heads:].astype(jnp.int32)
    columns = []
    for g in range(groups):
        mine = whole[:, g * per_group : (g + 1) * per_group]
        columns += [mine >> 16, (mine >> 8) & 255, mine & 255, jnp.zeros_like(mine)]
    pieces_ref[...] = jnp.concatenate(columns, axis=1).astype(f32).astype(bf16)
    for g in range(groups):
        cols = slice(g * NSTATE, (g + 1) * NSTATE)
        writes = b_ref[:, cols].astype(f32)
        bt_ref[cols, :] = jnp.where(odd, pltpu.roll(writes, NSTATE // 2, 1), writes).T.astype(bf16)
    totals = jnp.concatenate(
        [whole[(s + 1) * SUB - 1 : (s + 1) * SUB] for s in range(NSUB)], axis=0
    ).astype(f32)
    empty = jnp.zeros((2, heads), f32)
    small = jnp.concatenate([rate_ref[...], bypass_ref[...], totals, empty], axis=0)
    wide = jnp.dot(small, spread, precision=lax.Precision.HIGHEST, preferred_element_type=f32)
    rate = wide[0:1] * (-LOG2E / 1024.0)
    base = jnp.zeros_like(rate)
    rows_ref[0:1, :] = rate
    rows_ref[1:2, :] = wide[1:2]
    for s in range(NSUB):
        total = wide[2 + s : 3 + s]
        rows_ref[2 + s : 3 + s, :] = jnp.exp2(rate * total)
        rows_ref[8 + s : 9 + s, :] = jnp.exp2(rate * base)
        base = base + total
    decay_ref[...] = jnp.exp2(rate * base)
    rows_ref[6:8, :] = jnp.zeros((2, width), f32)
    rows_ref[12:16, :] = jnp.zeros((4, width), f32)
    taps_ref[0:KERNEL, :] = 0.5 * w_ref[...].astype(f32)
    bias = 0.5 * bias_ref[...].astype(f32)
    taps_ref[KERNEL : KERNEL + 1, :] = jnp.concatenate([bias[k : k + 1] for k in range(width // 128)], axis=1)
    taps_ref[KERNEL + 1 :, :] = jnp.zeros((7 - KERNEL, width), f32)


def mixing_kernel(pieces_ref, bt_ref, c_ref, left_ref, right_ref, scores_ref, ct_ref):
    groups = c_ref.shape[1] // NSTATE
    heads = pieces_ref.shape[1] // 4
    per_group = heads // groups
    row = iota((4 * heads, 16 * heads), 0)
    col = iota((4 * heads, 16 * heads), 1)
    kind = col & 15
    part = (row >> bits(per_group)) & 3
    row_head = ((row >> bits(4 * per_group)) << bits(per_group)) | (row & (per_group - 1))
    same = (row_head == (col >> 4)) & (part < 3)
    to_left = jnp.where(same & (part == kind), 1.0, 0.0).astype(bf16)
    scale = jnp.where(kind == 3, -65536.0, jnp.where(kind == 4, -256.0, -1.0))
    to_right = jnp.where(same & (part == kind - 3), scale, 0.0).astype(bf16)
    col_kind = iota((1, 16 * heads), 1) & 15
    ones = jnp.where((col_kind >= 3) & (col_kind < 6), 1.0, 0.0)
    fixed = jnp.where(col_kind == 0, 65536.0, jnp.where(col_kind == 1, 256.0, jnp.where(col_kind == 2, 1.0, 0.0)))
    pieces = pieces_ref[...]
    left_ref[...] = (dot(pieces, to_left) + ones).astype(bf16)
    right_ref[...] = (dot(pieces, to_right) + fixed).T.astype(bf16)
    odd = (lax.axis_index("ctx") & 1) == 1
    causal = iota((SUB, SUB), 0) >= iota((SUB, SUB), 1)
    for g in range(groups):
        cols = slice(g * NSTATE, (g + 1) * NSTATE)
        reads = c_ref[:, cols].astype(f32)
        reads = jnp.where(odd, pltpu.roll(reads, NSTATE // 2, 1), reads).astype(bf16)
        ct_ref[:, cols] = reads
        for s in range(NSUB):
            rows = slice(s * SUB, (s + 1) * SUB)
            scores_ref[g, rows, :] = jnp.where(causal, dot(reads[rows], bt_ref[cols, rows]), 0.0)


def state_kernel(decay_in, x_ref, tail_ref, taps_ref, pieces_ref, spread_ref, bt_ref, rows_ref, f_ref, local_ref, own_ref, given_ref, decay_ref):
    half = NSTATE // 2
    decay_ref[...] = decay_in[...]
    for t in range(LANES // TILE):
        cols = slice(t * TILE, (t + 1) * TILE)
        taps = taps_ref[:, cols]
        rate = rows_ref[0:1, cols]
        running = None
        for s in range(NSUB):
            rows = slice(s * SUB, (s + 1) * SUB)
            if s == 0:
                before = tail_ref[:, cols].astype(f32)
            else:
                before = x_ref[s * SUB - 16 : s * SUB, cols].astype(f32)[16 - TAIL :]
            current = x_ref[rows, cols].astype(f32)
            padded = jnp.concatenate([before, current], axis=0)
            summed = taps[KERNEL : KERNEL + 1] + taps[KERNEL - 1 : KERNEL] * current
            for back in range(1, KERNEL):
                moved = pltpu.roll(padded, back, 0)[TAIL:]
                summed = summed + taps[KERNEL - 1 - back : KERNEL - back] * moved
            filtered = silu_of_twice(summed).astype(bf16)
            f_ref[rows, cols] = filtered
            wide = dot(pieces_ref[rows, :], spread_ref[:, cols])
            weight = jnp.exp2(rate * (wide[SUB - 1 : SUB] - wide))
            weighted = (weight * filtered.astype(f32)).astype(bf16)
            part = dot(bt_ref[:, rows], weighted)
            running = part if s == 0 else rows_ref[2 + s : 3 + s, cols] * running + part
            if s < NSUB - 1:
                local_ref[s, :, cols] = running.astype(bf16)
        running = running.astype(bf16)
        own_ref[:, cols] = running[:half]
        given_ref[:, cols] = running[half:]


def inside_kernel(
    start, decay_in, z_ref, f_ref, local_ref, c_ref, pieces_ref, spread_ref, left_ref, right_ref, scores_ref, rows_ref,
    rate_ref, *refs,
):
    decay_ref, p_ref, g_ref, wall = refs[-4:]
    decay_ref[...] = decay_in[...]
    first_head = (start + pl.program_id(0) * ILANES) >> HEAD_SHIFT
    wall[...] = jnp.zeros_like(wall)
    first_lanes = iota((SUB, 128), 1) < HEAD_DIM
    for s in range(NSUB):
        rows = slice(s * SUB, (s + 1) * SUB)
        for q in range(ILANES // HEAD_DIM):
            wall[16 * q : 16 * q + 16, q * SUB : (q + 1) * SUB] = right_ref[16 * q : 16 * q + 16, rows]
        scores = scores_ref[0, rows, :]
        left = left_ref[rows, :]
        pieces = pieces_ref[rows, :]
        reads = c_ref[rows, :]
        for r in range(ILANES // TILE):
            cols = slice(r * TILE, (r + 1) * TILE)
            growth = jnp.exp2(rows_ref[0:1, cols] * dot(pieces, spread_ref[:, cols]))
            gate = silu_of_twice(0.5 * z_ref[rows, cols].astype(f32))
            g_ref[rows, cols] = (gate * growth * rows_ref[8 + s : 9 + s, cols]).astype(bf16)
            filtered = f_ref[rows, cols].astype(f32)
            total = rows_ref[1:2, cols] * filtered
            if s > 0:
                total = total + growth * dot(reads, local_ref[s - 1, :, cols])
            insides = []
            for q in range(2 * r, 2 * r + 2):
                spans = dot(left, wall[:, 2 * q * SUB : (2 * q + 2) * SUB])
                mixing = []
                for k in range(2):
                    scale = rate_ref[first_head + 2 * q + k] * (-LOG2E / 1024.0)
                    decays = jnp.exp2(jnp.maximum(spans[:, k * SUB : (k + 1) * SUB], 0.0) * scale)
                    mixing.append((decays * scores).astype(bf16))
                pair = filtered[:, 128 * (q - 2 * r) : 128 * (q - 2 * r) + 128]
                stacked = jnp.concatenate(
                    [jnp.where(first_lanes, pair, 0.0), jnp.where(first_lanes, 0.0, pair)], axis=0
                ).astype(bf16)
                insides.append(dot(jnp.concatenate(mixing, axis=1), stacked))
            p_ref[rows, cols] = ((total + jnp.concatenate(insides, axis=1)) * gate).astype(bf16)


def final_kernel(p_ref, g_ref, mine_ref, other_ref, c_ref, gain_ref, *rest):
    out_ref = rest[-1]
    same = (iota((TILE, TILE), 0) >> HEAD_SHIFT) == (iota((TILE, TILE), 1) >> HEAD_SHIFT)
    mean = jnp.where(same, 1.0 / HEAD_DIM, 0.0).astype(bf16)
    for t in range(out_ref.shape[1] // TILE):
        cols = slice(t * TILE, (t + 1) * TILE)
        entering = jnp.concatenate([mine_ref[:, cols], other_ref[:, cols]], axis=0)
        gain = gain_ref[:, cols]
        for s in range(NSUB):
            rows = slice(s * SUB, (s + 1) * SUB)
            carried = dot(c_ref[rows, :], entering)
            gated = p_ref[rows, cols].astype(f32) + carried * g_ref[rows, cols].astype(f32)
            meansq = dot((gated * gated).astype(bf16), mean)
            out_ref[rows, cols] = (gated * lax.rsqrt(meansq + 1e-05) * gain).astype(bf16)


def full(shape):
    return pl.BlockSpec(shape, lambda *i: (0,) * len(shape))


def call(kernel, operands, in_specs, after=(), limit=16, cost=1, **kwargs):
    count = len(operands)

    def ordered(*refs):
        kernel(*refs[:count], *refs[count + len(after) :])

    return pl.pallas_call(
        ordered,
        in_specs=list(in_specs) + [pl.BlockSpec(memory_space=pl.ANY)] * len(after),
        compiler_params=pltpu.CompilerParams(vmem_limit_bytes=limit * MIB),
        cost_estimate=pl.CostEstimate(flops=1, bytes_accessed=cost, transcendentals=0),
        **kwargs,
    )(*operands, *after)


def per_device(
    features,
    output_switch,
    input_proj,
    output_proj,
    step_codes,
    head_rate,
    conv_weight,
    conv_bias,
    bypass_factor,
    norm_gain,
):
    tokens, width = features.shape
    heads = head_rate.shape[0]
    groups = input_proj.shape[1] // NSTATE
    assert tokens == BLOCK and width == heads * HEAD_DIM
    runs = lax.axis_size("ctx")
    pairs = runs // 2
    swap = [(i, i ^ 1) for i in range(runs)]

    def shape(dims, dtype):
        return jax.ShapeDtypeStruct(dims, dtype)

    group_width = width // groups
    per_group = heads // groups
    half = NSTATE // 2
    assert sum(WIDTHS) == width
    hbm = pl.BlockSpec(memory_space=pltpu.HBM)

    last_rows = features[tokens - TAIL :]
    tail = lax.ppermute(last_rows, "ctx", [(i, i + 1) for i in range(runs - 1)])
    prepared = (
        ((tokens, 4 * heads), bf16),
        ((4 * per_group, group_width), bf16),
        ((groups * NSTATE, tokens), bf16),
        ((16, width), f32),
        ((8, width), f32),
        ((1, width), f32),
        ((1, width), f32),
    )
    pieces, spread, bt, rows, taps, decay, parity = call(
        prep_kernel,
        (
            step_codes.T, head_rate[None], bypass_factor[None], input_proj, conv_weight,
            conv_bias.reshape(width // 128, 128),
        ),
        [hbm] * 6,
        after=(last_rows,),
        limit=PREP_LIMIT,
        cost=PREP_BYTES,
        grid=(1,),
        out_specs=[full(dims) for dims, _ in prepared],
        out_shape=[shape(*kind) for kind in prepared],
        scratch_shapes=[
            pltpu.VMEM((heads, tokens), jnp.int32),
            pltpu.VMEM((1, heads), f32),
            pltpu.VMEM((1, heads), f32),
            pltpu.VMEM((tokens, groups * NSTATE), bf16),
            pltpu.VMEM((KERNEL, width), bf16),
            pltpu.VMEM((width // 128, 128), bf16),
            pltpu.SemaphoreType.DMA((6,)),
        ],
    )

    def mixing_parts(after):
        kinds = (
            ((tokens, 16 * heads), bf16),
            ((16 * heads, tokens), bf16),
            ((groups, tokens, SUB), f32),
            ((tokens, groups * NSTATE), bf16),
        )
        return call(
            mixing_kernel,
            (pieces, bt, output_proj),
            [full((tokens, 4 * heads)), full((groups * NSTATE, tokens)), full((tokens, groups * NSTATE))],
            after,
            grid=(1,),
            out_specs=[full(dims) for dims, _ in kinds],
            out_shape=[shape(*kind) for kind in kinds],
        )

    gain = norm_gain[None]

    def conv_states(start, lanes, decay, after):
        first = start // LANES
        column = lambda i: (0, first + i)
        group = lambda i: (first + i) * LANES // group_width
        mine = lambda i: (0, i)
        return call(
            state_kernel,
            (decay, features, tail, taps, pieces, spread, bt, rows),
            [
                full((1, width)),
                pl.BlockSpec((tokens, LANES), column),
                pl.BlockSpec((TAIL, LANES), column),
                pl.BlockSpec((8, LANES), column),
                pl.BlockSpec((tokens, 4 * per_group), lambda i: (0, group(i))),
                pl.BlockSpec((4 * per_group, LANES), lambda i: (0, (first + i) % (group_width // LANES))),
                pl.BlockSpec((NSTATE, tokens), lambda i: (group(i), 0)),
                pl.BlockSpec((16, LANES), column),
            ],
            after,
            limit=STATE_LIMIT,
            cost=STATE_BYTES,
            grid=(lanes // LANES,),
            out_specs=[
                pl.BlockSpec((tokens, LANES), mine),
                pl.BlockSpec((NSUB - 1, NSTATE, LANES), lambda i: (0, 0, i)),
                pl.BlockSpec((half, LANES), mine),
                pl.BlockSpec((half, LANES), mine),
                full((1, width)),
            ],
            out_shape=(
                shape((tokens, lanes), bf16),
                shape((NSUB - 1, NSTATE, lanes), bf16),
                shape((half, lanes), bf16),
                shape((half, lanes), bf16),
                shape((1, width), f32),
            ),
        )

    def inside(start, lanes, inner, whole, filtered, local, filled, decay, after):
        first = start // ILANES
        skip = inner // ILANES
        heads_here = ILANES // HEAD_DIM
        column = lambda i: (0, first + i)
        group = lambda i: (first + i) * ILANES // group_width
        mine = lambda i: (0, skip + i)
        return call(
            functools.partial(inside_kernel, start),
            (decay, output_switch, filtered, local, reads, pieces, spread, left, right, scores, rows, head_rate, *filled),
            [
                full((1, width)),
                pl.BlockSpec((tokens, ILANES), column),
                pl.BlockSpec((tokens, ILANES), mine),
                pl.BlockSpec((NSUB - 1, NSTATE, ILANES), lambda i: (0, 0, skip + i)),
                pl.BlockSpec((tokens, NSTATE), lambda i: (0, group(i))),
                pl.BlockSpec((tokens, 4 * per_group), lambda i: (0, group(i))),
                pl.BlockSpec((4 * per_group, ILANES), lambda i: (0, (first + i) % (group_width // ILANES))),
                pl.BlockSpec((tokens, 16 * heads_here), column),
                pl.BlockSpec((16 * heads_here, tokens), lambda i: (first + i, 0)),
                pl.BlockSpec((1, tokens, SUB), lambda i: (group(i), 0, 0)),
                pl.BlockSpec((16, ILANES), column),
                pl.BlockSpec(memory_space=pltpu.SMEM),
            ]
            + [pl.BlockSpec(memory_space=pl.ANY)] * len(filled),
            after,
            limit=INSIDE_LIMIT,
            cost=INSIDE_BYTES,
            grid=(lanes // ILANES,),
            out_specs=[full((1, width))] + [pl.BlockSpec((tokens, ILANES), mine)] * 2,
            out_shape=(shape((1, width), f32), shape((tokens, whole), bf16), shape((tokens, whole), bf16)),
            input_output_aliases={12: 1, 13: 2} if filled else {},
            scratch_shapes=[pltpu.VMEM((16 * heads_here, heads_here * SUB), bf16)],
        )

    def final(start, lanes, inner, out, kept, growth, own, other, after):
        block = FLANES if start % FLANES == 0 and lanes % FLANES == 0 else LANES
        first = start // block
        skip = inner // block
        column = lambda i: (0, first + i)
        mine = lambda i: (0, i)
        operands = [kept, growth, own, other, reads, gain]
        in_specs = [
            pl.BlockSpec((tokens, block), mine),
            pl.BlockSpec((tokens, block), mine),
            pl.BlockSpec((half, block), lambda i: (0, skip + i)),
            pl.BlockSpec((half, block), lambda i: (0, skip + i)),
            pl.BlockSpec((tokens, NSTATE), lambda i: (0, (first + i) * block // group_width)),
            pl.BlockSpec((1, block), column),
        ]
        aliases = {}
        if out is not None:
            aliases = {len(operands): 0}
            operands.append(out)
            in_specs.append(pl.BlockSpec(memory_space=pl.ANY))
        return call(
            final_kernel,
            operands,
            in_specs,
            after,
            limit=FINAL_LIMIT,
            cost=FINAL_BYTES,
            grid=(lanes // block,),
            out_specs=pl.BlockSpec((tokens, block), column),
            out_shape=shape((tokens, width), bf16),
            input_output_aliases=aliases,
        )

    def carry(c, own, given):
        cols = slice(starts[c], starts[c] + WIDTHS[c])
        got = lax.ppermute(given, "ctx", swap)
        yield given

        odd = parity[:, cols] > 0.5

        def coefficients():
            mine, theirs = now["decay"][:, cols], now["other"][:, cols]
            return jnp.where(odd, theirs, mine), jnp.where(odd, mine, theirs)

        own, got = own.astype(f32), got.astype(f32)
        before, behind = jnp.where(odd, got, own), jnp.where(odd, own, got)
        entering = None
        for step in range(pairs - 1):
            even, later = coefficients()
            sent = before if entering is None else even * entering + before
            sent = (later * sent + behind).astype(bf16)
            route = [(2 * step + k, 2 * step + 2 + k) for k in range(2)]
            arrived = lax.ppermute(sent, "ctx", route).astype(f32)
            yield sent
            entering = arrived if entering is None else entering + arrived
        even, later = coefficients()
        between = before if entering is None else even * entering + before
        entering = jnp.zeros_like(between) if entering is None else entering
        mine = jnp.where(odd, between, entering).astype(bf16)
        given = jnp.where(odd, entering, between).astype(bf16)
        other = lax.ppermute(given, "ctx", swap)
        yield given
        yield mine, other

    starts = [sum(WIDTHS[:c]) for c in range(len(WIDTHS))]
    now = {"decay": decay}
    travel, entering, remaining = [], {}, []

    def advance():
        waited = []
        for c, steps in enumerate(travel):
            if remaining[c]:
                value = next(steps)
                remaining[c] -= 1
                if remaining[c]:
                    waited.append(value)
                else:
                    entering[c] = value
        return tuple(waited)

    def splits(lanes):
        return [(k, min(IWIDTH, lanes - k)) for k in range(0, lanes, IWIDTH)]

    made, token = [], ()
    for c, lanes in enumerate(WIDTHS):
        made.append(conv_states(starts[c], lanes, now["decay"], token))
        now["decay"] = made[c][4]
        if c == 0:
            now["other"] = lax.ppermute(now["decay"], "ctx", swap)
        travel.append(carry(c, made[c][2], made[c][3]))
        remaining.append(pairs + 2)
        token = advance()
    left, right, scores, reads = mixing_parts(token)
    token = token[:-1] + (reads,)
    kept = []
    for c, lanes in enumerate(WIDTHS):
        filled = ()
        for inner, size in splits(lanes):
            now["decay"], *filled = inside(
                starts[c] + inner, size, inner, lanes, made[c][0], made[c][1], filled, now["decay"], token
            )
            token = advance()
        kept.append(filled)
    out = None
    for c, lanes in enumerate(WIDTHS):
        while c not in entering:
            token = advance()
        out = final(starts[c], lanes, 0, out, *kept[c], *entering[c], token)
        token = advance()
    return out


def solution(mesh):
    placed = (
        P(("groups", "ctx"), "head"),
        P(("groups", "ctx"), "head"),
        P(("groups", "ctx"), "head"),
        P(("groups", "ctx"), "head"),
        P(("groups", "ctx"), "head"),
        P("head"),
        P(None, "head"),
        P("head"),
        P("head"),
        P("head"),
    )
    return jax.shard_map(
        per_device,
        mesh=mesh,
        in_specs=placed,
        out_specs=P(("groups", "ctx"), "head"),
        check_vma=False,
    )
```

```python
import functools
import math

import jax
import jax.numpy as jnp
from jax import lax
from jax.experimental import pallas as pl
from jax.experimental.pallas import tpu as pltpu
from jax.sharding import PartitionSpec as P

NSTATE = 128
KERNEL = 4
BLOCK = 512
HEAD_DIM = 64
SUB = 128
NSUB = BLOCK // SUB
WIDTHS = (2048, 2048)
HEAD_SHIFT = 6
LANES = 512
ILANES = 512
FLANES = 1024
TILE = 256
IWIDTH = 1024
TAIL = 8

f32 = jnp.float32
bf16 = jnp.bfloat16
LOG2E = math.log2(math.e)
MIB = 1024 * 1024
PREP_LIMIT, STATE_LIMIT, INSIDE_LIMIT, FINAL_LIMIT = 16, 16, 16, 16
TAIL_BYTES, PREP_BYTES, STATE_BYTES, INSIDE_BYTES, FINAL_BYTES = 16 << 20, 1, 1, 1, 1


def iota(shape, axis):
    return lax.broadcasted_iota(jnp.int32, shape, axis)


def dot(a, b):
    return jnp.dot(a, b, preferred_element_type=f32)


def silu_of_twice(values):
    return values + values * jnp.tanh(values)


def bits(size):
    return size.bit_length() - 1


def prep_kernel(
    codes_hbm, rate_hbm, bypass_hbm, b_hbm, w_hbm, bias_hbm,
    pieces_ref, spread_ref, bt_ref, rows_ref, taps_ref, decay_ref, odd_ref,
    codes_ref, rate_ref, bypass_ref, b_ref, w_ref, bias_ref, sems,
):
    pairs = (
        (codes_hbm, codes_ref), (rate_hbm, rate_ref), (bypass_hbm, bypass_ref), (b_hbm, b_ref),
        (w_hbm, w_ref), (bias_hbm, bias_ref),
    )
    copies = [pltpu.make_async_copy(a, b, sems.at[k]) for k, (a, b) in enumerate(pairs)]
    for copy in copies:
        copy.start()
    heads, tokens = codes_ref.shape
    width = rows_ref.shape[1]
    groups = b_ref.shape[1] // NSTATE
    per_group = heads // groups
    group_width = width // groups
    causal = iota((SUB, SUB), 0) >= iota((SUB, SUB), 1)
    lower = jnp.where(causal, 1.0, 0.0).astype(bf16)
    row = iota((4 * per_group, group_width), 0)
    part = row >> bits(per_group)
    hit = (row & (per_group - 1)) == (iota((4 * per_group, group_width), 1) >> HEAD_SHIFT)
    scale = jnp.where(part == 0, 65536.0, jnp.where(part == 1, 256.0, jnp.where(part == 2, 1.0, 0.0)))
    spread_ref[...] = jnp.where(hit, scale, 0.0).astype(bf16)
    odd = (lax.axis_index("ctx") & 1) == 1
    odd_ref[...] = jnp.where(odd, jnp.ones(odd_ref.shape, f32), 0.0)
    spread = jnp.where(iota((heads, width), 0) == (iota((heads, width), 1) >> HEAD_SHIFT), 1.0, 0.0)
    for copy in copies:
        copy.wait()
    codes = codes_ref[...].T
    split = jnp.concatenate([codes >> 8, codes & 255], axis=1).astype(f32).astype(bf16)
    sums = jnp.concatenate([dot(lower, split[s * SUB : (s + 1) * SUB]) for s in range(NSUB)], axis=0)
    whole = sums[:, :heads].astype(jnp.int32) * 256 + sums[:, heads:].astype(jnp.int32)
    columns = []
    for g in range(groups):
        mine = whole[:, g * per_group : (g + 1) * per_group]
        columns += [mine >> 16, (mine >> 8) & 255, mine & 255, jnp.zeros_like(mine)]
    pieces_ref[...] = jnp.concatenate(columns, axis=1).astype(f32).astype(bf16)
    for g in range(groups):
        cols = slice(g * NSTATE, (g + 1) * NSTATE)
        writes = b_ref[:, cols].astype(f32)
        bt_ref[cols, :] = jnp.where(odd, pltpu.roll(writes, NSTATE // 2, 1), writes).T.astype(bf16)
    totals = jnp.concatenate(
        [whole[(s + 1) * SUB - 1 : (s + 1) * SUB] for s in range(NSUB)], axis=0
    ).astype(f32)
    empty = jnp.zeros((2, heads), f32)
    small = jnp.concatenate([rate_ref[...], bypass_ref[...], totals, empty], axis=0)
    wide = jnp.dot(small, spread, precision=lax.Precision.HIGHEST, preferred_element_type=f32)
    rate = wide[0:1] * (-LOG2E / 1024.0)
    base = jnp.zeros_like(rate)
    rows_ref[0:1, :] = rate
    rows_ref[1:2, :] = wide[1:2]
    for s in range(NSUB):
        total = wide[2 + s : 3 + s]
        rows_ref[2 + s : 3 + s, :] = jnp.exp2(rate * total)
        rows_ref[8 + s : 9 + s, :] = jnp.exp2(rate * base)
        base = base + total
    decay_ref[...] = jnp.exp2(rate * base)
    rows_ref[6:8, :] = jnp.zeros((2, width), f32)
    rows_ref[12:16, :] = jnp.zeros((4, width), f32)
    taps_ref[0:KERNEL, :] = 0.5 * w_ref[...].astype(f32)
    bias = 0.5 * bias_ref[...].astype(f32)
    taps_ref[KERNEL : KERNEL + 1, :] = jnp.concatenate([bias[k : k + 1] for k in range(width // 128)], axis=1)
    taps_ref[KERNEL + 1 :, :] = jnp.zeros((7 - KERNEL, width), f32)


def mixing_kernel(decay_in, pieces_ref, bt_ref, c_ref, left_ref, right_ref, scores_ref, ct_ref, decay_ref):
    decay_ref[...] = decay_in[...]
    groups = c_ref.shape[1] // NSTATE
    heads = pieces_ref.shape[1] // 4
    per_group = heads // groups
    row = iota((4 * heads, 16 * heads), 0)
    col = iota((4 * heads, 16 * heads), 1)
    kind = col & 15
    part = (row >> bits(per_group)) & 3
    row_head = ((row >> bits(4 * per_group)) << bits(per_group)) | (row & (per_group - 1))
    same = (row_head == (col >> 4)) & (part < 3)
    to_left = jnp.where(same & (part == kind), 1.0, 0.0).astype(bf16)
    scale = jnp.where(kind == 3, -65536.0, jnp.where(kind == 4, -256.0, -1.0))
    to_right = jnp.where(same & (part == kind - 3), scale, 0.0).astype(bf16)
    col_kind = iota((1, 16 * heads), 1) & 15
    ones = jnp.where((col_kind >= 3) & (col_kind < 6), 1.0, 0.0)
    fixed = jnp.where(col_kind == 0, 65536.0, jnp.where(col_kind == 1, 256.0, jnp.where(col_kind == 2, 1.0, 0.0)))
    pieces = pieces_ref[...]
    left_ref[...] = (dot(pieces, to_left) + ones).astype(bf16)
    right_ref[...] = (dot(pieces, to_right) + fixed).T.astype(bf16)
    odd = (lax.axis_index("ctx") & 1) == 1
    causal = iota((SUB, SUB), 0) >= iota((SUB, SUB), 1)
    for g in range(groups):
        cols = slice(g * NSTATE, (g + 1) * NSTATE)
        reads = c_ref[:, cols].astype(f32)
        reads = jnp.where(odd, pltpu.roll(reads, NSTATE // 2, 1), reads).astype(bf16)
        ct_ref[:, cols] = reads
        for s in range(NSUB):
            rows = slice(s * SUB, (s + 1) * SUB)
            scores_ref[g, rows, :] = jnp.where(causal, dot(reads[rows], bt_ref[cols, rows]), 0.0)


def state_kernel(start, decay_in, x_ref, tail_ref, taps_ref, pieces_ref, spread_ref, bt_ref, rows_ref, f_ref, local_ref, own_ref, given_ref, decay_ref):
    half = NSTATE // 2
    group_width = x_ref.shape[1] // (bt_ref.shape[0] // NSTATE)
    decay_ref[...] = decay_in[...]
    for t in range(f_ref.shape[1] // TILE):
        here = slice(t * TILE, (t + 1) * TILE)
        lane = start + t * TILE
        cols = slice(lane, lane + TILE)
        inner = slice(lane % group_width, lane % group_width + TILE)
        mine = slice(lane // group_width * NSTATE, (lane // group_width + 1) * NSTATE)
        taps = taps_ref[:, cols]
        rate = rows_ref[0:1, cols]
        running = None
        for s in range(NSUB):
            rows = slice(s * SUB, (s + 1) * SUB)
            if s == 0:
                before = tail_ref[:, cols].astype(f32)
            else:
                before = x_ref[s * SUB - 16 : s * SUB, cols].astype(f32)[16 - TAIL :]
            current = x_ref[rows, cols].astype(f32)
            padded = jnp.concatenate([before, current], axis=0)
            summed = taps[KERNEL : KERNEL + 1] + taps[KERNEL - 1 : KERNEL] * current
            for back in range(1, KERNEL):
                moved = pltpu.roll(padded, back, 0)[TAIL:]
                summed = summed + taps[KERNEL - 1 - back : KERNEL - back] * moved
            filtered = silu_of_twice(summed).astype(bf16)
            f_ref[rows, here] = filtered
            wide = dot(pieces_ref[rows, mine], spread_ref[:, inner])
            weight = jnp.exp2(rate * (wide[SUB - 1 : SUB] - wide))
            weighted = (weight * filtered.astype(f32)).astype(bf16)
            part = dot(bt_ref[mine, rows], weighted)
            running = part if s == 0 else rows_ref[2 + s : 3 + s, cols] * running + part
            if s < NSUB - 1:
                local_ref[s, :, here] = running.astype(bf16)
        running = running.astype(bf16)
        own_ref[:, here] = running[:half]
        given_ref[:, here] = running[half:]


def inside_kernel(
    start, skip, size, decay_in, z_ref, f_ref, local_ref, c_ref, pieces_ref, spread_ref, left_ref, right_ref,
    scores_ref, rows_ref, rate_ref, *refs,
):
    decay_ref, p_ref, g_ref, wall = refs[-4:]
    decay_ref[...] = decay_in[...]
    group_width = z_ref.shape[1] // (c_ref.shape[1] // NSTATE)
    wall[...] = jnp.zeros_like(wall)
    first_lanes = iota((SUB, 128), 1) < HEAD_DIM
    for b in range(size // ILANES):
        lane = start + b * ILANES
        group = lane // group_width
        mine = slice(group * NSTATE, (group + 1) * NSTATE)
        place = lane // HEAD_DIM * 16
        for s in range(NSUB):
            rows = slice(s * SUB, (s + 1) * SUB)
            for q in range(ILANES // HEAD_DIM):
                wall[16 * q : 16 * q + 16, q * SUB : (q + 1) * SUB] = right_ref[place + 16 * q : place + 16 * q + 16, rows]
            scores = scores_ref[group, rows, :]
            left = left_ref[rows, place : place + ILANES // HEAD_DIM * 16]
            pieces = pieces_ref[rows, mine]
            reads = c_ref[rows, mine]
            for r in range(ILANES // TILE):
                first = lane + r * TILE
                cols = slice(first, first + TILE)
                here = slice(skip + b * ILANES + r * TILE, skip + b * ILANES + (r + 1) * TILE)
                inner = slice(first % group_width, first % group_width + TILE)
                growth = jnp.exp2(rows_ref[0:1, cols] * dot(pieces, spread_ref[:, inner]))
                gate = silu_of_twice(0.5 * z_ref[rows, cols].astype(f32))
                g_ref[rows, here] = (gate * growth * rows_ref[8 + s : 9 + s, cols]).astype(bf16)
                filtered = f_ref[rows, here].astype(f32)
                total = rows_ref[1:2, cols] * filtered
                if s > 0:
                    total = total + growth * dot(reads, local_ref[s - 1, :, here])
                insides = []
                for q in range(2):
                    base = 2 * (2 * r + q)
                    spans = dot(left, wall[:, base * SUB : (base + 2) * SUB])
                    mixing = []
                    for k in range(2):
                        scale = rate_ref[lane // HEAD_DIM + base + k] * (-LOG2E / 1024.0)
                        decays = jnp.exp2(jnp.maximum(spans[:, k * SUB : (k + 1) * SUB], 0.0) * scale)
                        mixing.append((decays * scores).astype(bf16))
                    pair = filtered[:, 128 * q : 128 * q + 128]
                    stacked = jnp.concatenate(
                        [jnp.where(first_lanes, pair, 0.0), jnp.where(first_lanes, 0.0, pair)], axis=0
                    ).astype(bf16)
                    insides.append(dot(jnp.concatenate(mixing, axis=1), stacked))
                p_ref[rows, here] = ((total + jnp.concatenate(insides, axis=1)) * gate).astype(bf16)


def final_kernel(p_ref, g_ref, mine_ref, other_ref, c_ref, gain_ref, *rest):
    out_ref = rest[-1]
    same = (iota((TILE, TILE), 0) >> HEAD_SHIFT) == (iota((TILE, TILE), 1) >> HEAD_SHIFT)
    mean = jnp.where(same, 1.0 / HEAD_DIM, 0.0).astype(bf16)
    for t in range(out_ref.shape[1] // TILE):
        cols = slice(t * TILE, (t + 1) * TILE)
        here = pl.ds(pl.multiple_of(pl.program_id(0) * out_ref.shape[1] + t * TILE, TILE), TILE)
        entering = jnp.concatenate([mine_ref[:, here], other_ref[:, here]], axis=0)
        gain = gain_ref[:, cols]
        for s in range(NSUB):
            rows = slice(s * SUB, (s + 1) * SUB)
            carried = dot(c_ref[rows, :], entering)
            gated = p_ref[rows, here].astype(f32) + carried * g_ref[rows, here].astype(f32)
            meansq = dot((gated * gated).astype(bf16), mean)
            out_ref[rows, cols] = (gated * lax.rsqrt(meansq + 1e-05) * gain).astype(bf16)


def full(shape):
    return pl.BlockSpec(shape, lambda *i: (0,) * len(shape))


def call(kernel, operands, in_specs, after=(), limit=16, cost=1, **kwargs):
    count = len(operands)

    def ordered(*refs):
        kernel(*refs[:count], *refs[count + len(after) :])

    return pl.pallas_call(
        ordered,
        in_specs=list(in_specs) + [pl.BlockSpec(memory_space=pl.ANY)] * len(after),
        compiler_params=pltpu.CompilerParams(vmem_limit_bytes=limit * MIB),
        cost_estimate=pl.CostEstimate(flops=1, bytes_accessed=cost, transcendentals=0),
        **kwargs,
    )(*operands, *after)


def per_device(
    features,
    output_switch,
    input_proj,
    output_proj,
    step_codes,
    head_rate,
    conv_weight,
    conv_bias,
    bypass_factor,
    norm_gain,
):
    tokens, width = features.shape
    heads = head_rate.shape[0]
    groups = input_proj.shape[1] // NSTATE
    assert tokens == BLOCK and width == heads * HEAD_DIM
    runs = lax.axis_size("ctx")
    pairs = runs // 2
    swap = [(i, i ^ 1) for i in range(runs)]

    def shape(dims, dtype):
        return jax.ShapeDtypeStruct(dims, dtype)

    group_width = width // groups
    per_group = heads // groups
    half = NSTATE // 2
    assert sum(WIDTHS) == width
    hbm = pl.BlockSpec(memory_space=pltpu.HBM)

    def last_rows_kernel(x_ref, out_ref):
        out_ref[...] = x_ref[...].astype(f32)[16 - TAIL :].astype(bf16)

    last_rows = call(
        last_rows_kernel,
        (features,),
        [pl.BlockSpec((16, width), lambda i: (tokens // 16 - 1, 0))],
        limit=16,
        cost=TAIL_BYTES,
        grid=(1,),
        out_specs=full((TAIL, width)),
        out_shape=shape((TAIL, width), bf16),
    )
    tail = lax.ppermute(last_rows, "ctx", [(i, i + 1) for i in range(runs - 1)])
    prepared = (
        ((tokens, 4 * heads), bf16),
        ((4 * per_group, group_width), bf16),
        ((groups * NSTATE, tokens), bf16),
        ((16, width), f32),
        ((8, width), f32),
        ((1, width), f32),
        ((1, width), f32),
    )
    pieces, spread, bt, rows, taps, decay, parity = call(
        prep_kernel,
        (
            step_codes.T, head_rate[None], bypass_factor[None], input_proj, conv_weight,
            conv_bias.reshape(width // 128, 128),
        ),
        [hbm] * 6,
        after=(last_rows,),
        limit=PREP_LIMIT,
        cost=PREP_BYTES,
        grid=(1,),
        out_specs=[full(dims) for dims, _ in prepared],
        out_shape=[shape(*kind) for kind in prepared],
        scratch_shapes=[
            pltpu.VMEM((heads, tokens), jnp.int32),
            pltpu.VMEM((1, heads), f32),
            pltpu.VMEM((1, heads), f32),
            pltpu.VMEM((tokens, groups * NSTATE), bf16),
            pltpu.VMEM((KERNEL, width), bf16),
            pltpu.VMEM((width // 128, 128), bf16),
            pltpu.SemaphoreType.DMA((6,)),
        ],
    )

    def mixing_parts(decay, after):
        kinds = (
            ((tokens, 16 * heads), bf16),
            ((16 * heads, tokens), bf16),
            ((groups, tokens, SUB), f32),
            ((tokens, groups * NSTATE), bf16),
            ((1, width), f32),
        )
        return call(
            mixing_kernel,
            (decay, pieces, bt, output_proj),
            [full((1, width)), full((tokens, 4 * heads)), full((groups * NSTATE, tokens)), full((tokens, groups * NSTATE))],
            after,
            grid=(1,),
            out_specs=[full(dims) for dims, _ in kinds],
            out_shape=[shape(*kind) for kind in kinds],
        )

    gain = norm_gain[None]
    vmem = pl.BlockSpec(memory_space=pltpu.VMEM)

    def conv_states(start, lanes, decay, after):
        return call(
            functools.partial(state_kernel, start),
            (decay, features, tail, taps, pieces, spread, bt, rows),
            [vmem] * 8,
            after,
            limit=STATE_LIMIT,
            cost=STATE_BYTES,
            out_specs=[vmem] * 5,
            out_shape=(
                shape((tokens, lanes), bf16),
                shape((NSUB - 1, NSTATE, lanes), bf16),
                shape((half, lanes), bf16),
                shape((half, lanes), bf16),
                shape((1, width), f32),
            ),
        )

    def inside(start, lanes, inner, whole, filtered, local, filled, decay, after):
        heads_here = ILANES // HEAD_DIM
        return call(
            functools.partial(inside_kernel, start, inner, lanes),
            (decay, output_switch, filtered, local, reads, pieces, spread, left, right, scores, rows, head_rate, *filled),
            [vmem] * 11 + [pl.BlockSpec(memory_space=pltpu.SMEM)] + [vmem] * len(filled),
            after,
            limit=INSIDE_LIMIT,
            cost=INSIDE_BYTES,
            out_specs=[vmem] * 3,
            out_shape=(shape((1, width), f32), shape((tokens, whole), bf16), shape((tokens, whole), bf16)),
            input_output_aliases={12: 1, 13: 2} if filled else {},
            scratch_shapes=[pltpu.VMEM((16 * heads_here, heads_here * SUB), bf16)],
        )

    def final(start, lanes, inner, out, kept, growth, own, other, after):
        block = FLANES if start % FLANES == 0 and lanes % FLANES == 0 else LANES
        first = start // block
        column = lambda i: (0, first + i)
        operands = [kept, growth, own, other, reads, gain]
        in_specs = [
            vmem,
            vmem,
            vmem,
            vmem,
            pl.BlockSpec((tokens, NSTATE), lambda i: (0, (first + i) * block // group_width)),
            pl.BlockSpec((1, block), column),
        ]
        aliases = {}
        if out is not None:
            aliases = {len(operands): 0}
            operands.append(out)
            in_specs.append(pl.BlockSpec(memory_space=pl.ANY))
        return call(
            final_kernel,
            operands,
            in_specs,
            after,
            limit=FINAL_LIMIT,
            cost=FINAL_BYTES,
            grid=(lanes // block,),
            out_specs=pl.BlockSpec((tokens, block), column),
            out_shape=shape((tokens, width), bf16),
            input_output_aliases=aliases,
        )

    def carry(c, own, given):
        cols = slice(starts[c], starts[c] + WIDTHS[c])
        got = lax.ppermute(given, "ctx", swap)
        yield given

        odd = parity[:, cols] > 0.5

        def coefficients():
            mine, theirs = now["decay"][:, cols], now["other"][:, cols]
            return jnp.where(odd, theirs, mine), jnp.where(odd, mine, theirs)

        own, got = own.astype(f32), got.astype(f32)
        before, behind = jnp.where(odd, got, own), jnp.where(odd, own, got)
        entering = None
        for step in range(pairs - 1):
            even, later = coefficients()
            sent = before if entering is None else even * entering + before
            sent = (later * sent + behind).astype(bf16)
            route = [(2 * step + k, 2 * step + 2 + k) for k in range(2)]
            arrived = lax.ppermute(sent, "ctx", route).astype(f32)
            yield sent
            entering = arrived if entering is None else entering + arrived
        even, later = coefficients()
        between = before if entering is None else even * entering + before
        entering = jnp.zeros_like(between) if entering is None else entering
        mine = jnp.where(odd, between, entering).astype(bf16)
        given = jnp.where(odd, entering, between).astype(bf16)
        other = lax.ppermute(given, "ctx", swap)
        yield given
        yield mine, other

    starts = [sum(WIDTHS[:c]) for c in range(len(WIDTHS))]
    now = {"decay": decay}
    travel, entering, remaining = [], {}, []

    def advance(*chosen):
        waited = []
        for c, steps in enumerate(travel):
            if remaining[c] and c in (chosen or range(len(WIDTHS))):
                value = next(steps)
                remaining[c] -= 1
                if remaining[c]:
                    waited.append(value)
                else:
                    entering[c] = value
        return tuple(waited)

    def splits(lanes):
        return [(k, min(IWIDTH, lanes - k)) for k in range(0, lanes, IWIDTH)]

    made, token = [], ()
    for c, lanes in enumerate(WIDTHS):
        made.append(conv_states(starts[c], lanes, now["decay"], token))
        now["decay"] = made[c][4]
        if c == 0:
            now["other"] = lax.ppermute(now["decay"], "ctx", swap)
        travel.append(carry(c, made[c][2], made[c][3]))
        remaining.append(pairs + 2)
        token = advance(c)
    left, right, scores, reads, now["decay"] = mixing_parts(now["decay"], token)
    token = advance(*range(len(WIDTHS) - 1))
    calls = [(c, inner, size) for c, lanes in enumerate(WIDTHS) for inner, size in splits(lanes)]
    kept = [() for _ in WIDTHS]
    for k, (c, inner, size) in enumerate(calls):
        now["decay"], *kept[c] = inside(
            starts[c] + inner, size, inner, WIDTHS[c], made[c][0], made[c][1], kept[c], now["decay"], token
        )
        token = advance()
    out = None
    for c, lanes in enumerate(WIDTHS):
        while c not in entering:
            token = advance()
        out = final(starts[c], lanes, 0, out, *kept[c], *entering[c], token)
        token = advance()
    return out


def solution(mesh):
    placed = (
        P(("groups", "ctx"), "head"),
        P(("groups", "ctx"), "head"),
        P(("groups", "ctx"), "head"),
        P(("groups", "ctx"), "head"),
        P(("groups", "ctx"), "head"),
        P("head"),
        P(None, "head"),
        P("head"),
        P("head"),
        P("head"),
    )
    return jax.shard_map(
        per_device,
        mesh=mesh,
        in_specs=placed,
        out_specs=P(("groups", "ctx"), "head"),
        check_vma=False,
    )
```

```python
import functools
import math

import jax
import jax.numpy as jnp
from jax import lax
from jax.experimental import pallas as pl
from jax.experimental.pallas import tpu as pltpu
from jax.sharding import PartitionSpec as P

NSTATE = 128
KERNEL = 4
BLOCK = 512
HEAD_DIM = 64
SUB = 128
NSUB = BLOCK // SUB
WIDTHS = (2048, 2048)
HEAD_SHIFT = 6
LANES = 512
ILANES = 512
FLANES = 1024
TILE = 256
IWIDTH = 1024
TAIL = 8

f32 = jnp.float32
bf16 = jnp.bfloat16
LOG2E = math.log2(math.e)
MIB = 1024 * 1024
PREP_LIMIT, STATE_LIMIT, INSIDE_LIMIT, FINAL_LIMIT = 16, 16, 16, 16
TAIL_BYTES, PREP_BYTES, STATE_BYTES, INSIDE_BYTES, FINAL_BYTES = 16 << 20, 1, 1, 1, 1


def iota(shape, axis):
    return lax.broadcasted_iota(jnp.int32, shape, axis)


def dot(a, b):
    return jnp.dot(a, b, preferred_element_type=f32)


def silu_of_twice(values):
    return values + values * jnp.tanh(values)


def bits(size):
    return size.bit_length() - 1


def prep_kernel(
    codes_hbm, rate_hbm, bypass_hbm, b_hbm, w_hbm, bias_hbm,
    pieces_ref, spread_ref, bt_ref, rows_ref, taps_ref, decay_ref, odd_ref,
    codes_ref, rate_ref, bypass_ref, b_ref, w_ref, bias_ref, sems,
):
    pairs = (
        (codes_hbm, codes_ref), (rate_hbm, rate_ref), (bypass_hbm, bypass_ref), (b_hbm, b_ref),
        (w_hbm, w_ref), (bias_hbm, bias_ref),
    )
    copies = [pltpu.make_async_copy(a, b, sems.at[k]) for k, (a, b) in enumerate(pairs)]
    for copy in copies:
        copy.start()
    heads, tokens = codes_ref.shape
    width = rows_ref.shape[1]
    groups = b_ref.shape[1] // NSTATE
    per_group = heads // groups
    group_width = width // groups
    causal = iota((SUB, SUB), 0) >= iota((SUB, SUB), 1)
    lower = jnp.where(causal, 1.0, 0.0).astype(bf16)
    row = iota((4 * per_group, group_width), 0)
    part = row >> bits(per_group)
    hit = (row & (per_group - 1)) == (iota((4 * per_group, group_width), 1) >> HEAD_SHIFT)
    scale = jnp.where(part == 0, 65536.0, jnp.where(part == 1, 256.0, jnp.where(part == 2, 1.0, 0.0)))
    spread_ref[...] = jnp.where(hit, scale, 0.0).astype(bf16)
    odd = (lax.axis_index("ctx") & 1) == 1
    odd_ref[...] = jnp.where(odd, jnp.ones(odd_ref.shape, f32), 0.0)
    spread = jnp.where(iota((heads, width), 0) == (iota((heads, width), 1) >> HEAD_SHIFT), 1.0, 0.0)
    for copy in copies:
        copy.wait()
    codes = codes_ref[...].T
    split = jnp.concatenate([codes >> 8, codes & 255], axis=1).astype(f32).astype(bf16)
    sums = jnp.concatenate([dot(lower, split[s * SUB : (s + 1) * SUB]) for s in range(NSUB)], axis=0)
    whole = sums[:, :heads].astype(jnp.int32) * 256 + sums[:, heads:].astype(jnp.int32)
    columns = []
    for g in range(groups):
        mine = whole[:, g * per_group : (g + 1) * per_group]
        columns += [mine >> 16, (mine >> 8) & 255, mine & 255, jnp.zeros_like(mine)]
    pieces_ref[...] = jnp.concatenate(columns, axis=1).astype(f32).astype(bf16)
    for g in range(groups):
        cols = slice(g * NSTATE, (g + 1) * NSTATE)
        writes = b_ref[:, cols].astype(f32)
        bt_ref[cols, :] = jnp.where(odd, pltpu.roll(writes, NSTATE // 2, 1), writes).T.astype(bf16)
    totals = jnp.concatenate(
        [whole[(s + 1) * SUB - 1 : (s + 1) * SUB] for s in range(NSUB)], axis=0
    ).astype(f32)
    empty = jnp.zeros((2, heads), f32)
    small = jnp.concatenate([rate_ref[...], bypass_ref[...], totals, empty], axis=0)
    wide = jnp.dot(small, spread, precision=lax.Precision.HIGHEST, preferred_element_type=f32)
    rate = wide[0:1] * (-LOG2E / 1024.0)
    base = jnp.zeros_like(rate)
    rows_ref[0:1, :] = rate
    rows_ref[1:2, :] = wide[1:2]
    for s in range(NSUB):
        total = wide[2 + s : 3 + s]
        rows_ref[2 + s : 3 + s, :] = jnp.exp2(rate * total)
        rows_ref[8 + s : 9 + s, :] = jnp.exp2(rate * base)
        base = base + total
    decay_ref[...] = jnp.exp2(rate * base)
    rows_ref[6:8, :] = jnp.zeros((2, width), f32)
    rows_ref[12:16, :] = jnp.zeros((4, width), f32)
    taps_ref[0:KERNEL, :] = 0.5 * w_ref[...].astype(f32)
    bias = 0.5 * bias_ref[...].astype(f32)
    taps_ref[KERNEL : KERNEL + 1, :] = jnp.concatenate([bias[k : k + 1] for k in range(width // 128)], axis=1)
    taps_ref[KERNEL + 1 :, :] = jnp.zeros((7 - KERNEL, width), f32)


def mixing_kernel(decay_in, pieces_ref, bt_ref, c_ref, left_ref, right_ref, scores_ref, ct_ref, decay_ref):
    decay_ref[...] = decay_in[...]
    groups = c_ref.shape[1] // NSTATE
    heads = pieces_ref.shape[1] // 4
    per_group = heads // groups
    row = iota((4 * heads, 16 * heads), 0)
    col = iota((4 * heads, 16 * heads), 1)
    kind = col & 15
    part = (row >> bits(per_group)) & 3
    row_head = ((row >> bits(4 * per_group)) << bits(per_group)) | (row & (per_group - 1))
    same = (row_head == (col >> 4)) & (part < 3)
    to_left = jnp.where(same & (part == kind), 1.0, 0.0).astype(bf16)
    scale = jnp.where(kind == 3, -65536.0, jnp.where(kind == 4, -256.0, -1.0))
    to_right = jnp.where(same & (part == kind - 3), scale, 0.0).astype(bf16)
    col_kind = iota((1, 16 * heads), 1) & 15
    ones = jnp.where((col_kind >= 3) & (col_kind < 6), 1.0, 0.0)
    fixed = jnp.where(col_kind == 0, 65536.0, jnp.where(col_kind == 1, 256.0, jnp.where(col_kind == 2, 1.0, 0.0)))
    pieces = pieces_ref[...]
    left_ref[...] = (dot(pieces, to_left) + ones).astype(bf16)
    right_ref[...] = (dot(pieces, to_right) + fixed).T.astype(bf16)
    odd = (lax.axis_index("ctx") & 1) == 1
    causal = iota((SUB, SUB), 0) >= iota((SUB, SUB), 1)
    for g in range(groups):
        cols = slice(g * NSTATE, (g + 1) * NSTATE)
        reads = c_ref[:, cols].astype(f32)
        reads = jnp.where(odd, pltpu.roll(reads, NSTATE // 2, 1), reads).astype(bf16)
        ct_ref[:, cols] = reads
        for s in range(NSUB):
            rows = slice(s * SUB, (s + 1) * SUB)
            scores_ref[g, rows, :] = jnp.where(causal, dot(reads[rows], bt_ref[cols, rows]), 0.0)


def state_kernel(start, decay_in, x_ref, tail_ref, taps_ref, pieces_ref, spread_ref, bt_ref, rows_ref, f_ref, local_ref, own_ref, given_ref, decay_ref):
    half = NSTATE // 2
    group_width = x_ref.shape[1] // (bt_ref.shape[0] // NSTATE)
    decay_ref[...] = decay_in[...]
    for t in range(f_ref.shape[1] // TILE):
        here = slice(t * TILE, (t + 1) * TILE)
        lane = start + t * TILE
        cols = slice(lane, lane + TILE)
        inner = slice(lane % group_width, lane % group_width + TILE)
        mine = slice(lane // group_width * NSTATE, (lane // group_width + 1) * NSTATE)
        taps = taps_ref[:, cols]
        rate = rows_ref[0:1, cols]
        running = None
        for s in range(NSUB):
            rows = slice(s * SUB, (s + 1) * SUB)
            if s == 0:
                before = tail_ref[:, cols].astype(f32)
            else:
                before = x_ref[s * SUB - 16 : s * SUB, cols].astype(f32)[16 - TAIL :]
            current = x_ref[rows, cols].astype(f32)
            padded = jnp.concatenate([before, current], axis=0)
            summed = taps[KERNEL : KERNEL + 1] + taps[KERNEL - 1 : KERNEL] * current
            for back in range(1, KERNEL):
                moved = pltpu.roll(padded, back, 0)[TAIL:]
                summed = summed + taps[KERNEL - 1 - back : KERNEL - back] * moved
            filtered = silu_of_twice(summed).astype(bf16)
            f_ref[rows, here] = filtered
            wide = dot(pieces_ref[rows, mine], spread_ref[:, inner])
            weight = jnp.exp2(rate * (wide[SUB - 1 : SUB] - wide))
            weighted = weight.astype(bf16) * filtered
            part = dot(bt_ref[mine, rows], weighted)
            running = part if s == 0 else rows_ref[2 + s : 3 + s, cols] * running + part
            if s < NSUB - 1:
                local_ref[s, :, here] = running.astype(bf16)
        running = running.astype(bf16)
        own_ref[:, here] = running[:half]
        given_ref[:, here] = running[half:]


def inside_kernel(
    start, skip, size, decay_in, z_ref, f_ref, local_ref, c_ref, pieces_ref, spread_ref, left_ref, right_ref,
    scores_ref, rows_ref, rate_ref, *refs,
):
    decay_ref, p_ref, g_ref, wall = refs[-4:]
    decay_ref[...] = decay_in[...]
    group_width = z_ref.shape[1] // (c_ref.shape[1] // NSTATE)
    wall[...] = jnp.zeros_like(wall)
    first_lanes = iota((SUB, 128), 1) < HEAD_DIM
    for b in range(size // ILANES):
        lane = start + b * ILANES
        group = lane // group_width
        mine = slice(group * NSTATE, (group + 1) * NSTATE)
        place = lane // HEAD_DIM * 16
        for s in range(NSUB):
            rows = slice(s * SUB, (s + 1) * SUB)
            for q in range(ILANES // HEAD_DIM):
                wall[16 * q : 16 * q + 16, q * SUB : (q + 1) * SUB] = right_ref[place + 16 * q : place + 16 * q + 16, rows]
            scores = scores_ref[group, rows, :]
            left = left_ref[rows, place : place + ILANES // HEAD_DIM * 16]
            pieces = pieces_ref[rows, mine]
            reads = c_ref[rows, mine]
            for r in range(ILANES // TILE):
                first = lane + r * TILE
                cols = slice(first, first + TILE)
                here = slice(skip + b * ILANES + r * TILE, skip + b * ILANES + (r + 1) * TILE)
                inner = slice(first % group_width, first % group_width + TILE)
                growth = jnp.exp2(rows_ref[0:1, cols] * dot(pieces, spread_ref[:, inner]))
                gate = silu_of_twice(0.5 * z_ref[rows, cols].astype(f32))
                g_ref[rows, here] = (gate * growth * rows_ref[8 + s : 9 + s, cols]).astype(bf16)
                filtered = f_ref[rows, here].astype(f32)
                total = rows_ref[1:2, cols] * filtered
                if s > 0:
                    total = total + growth * dot(reads, local_ref[s - 1, :, here])
                insides = []
                for q in range(2):
                    base = 2 * (2 * r + q)
                    spans = dot(left, wall[:, base * SUB : (base + 2) * SUB])
                    mixing = []
                    for k in range(2):
                        scale = rate_ref[lane // HEAD_DIM + base + k] * (-LOG2E / 1024.0)
                        decays = jnp.exp2(jnp.maximum(spans[:, k * SUB : (k + 1) * SUB], 0.0) * scale)
                        mixing.append((decays * scores).astype(bf16))
                    pair = filtered[:, 128 * q : 128 * q + 128]
                    stacked = jnp.concatenate(
                        [jnp.where(first_lanes, pair, 0.0), jnp.where(first_lanes, 0.0, pair)], axis=0
                    ).astype(bf16)
                    insides.append(dot(jnp.concatenate(mixing, axis=1), stacked))
                p_ref[rows, here] = ((total + jnp.concatenate(insides, axis=1)) * gate).astype(bf16)


def final_kernel(p_ref, g_ref, mine_ref, other_ref, c_ref, gain_ref, *rest):
    out_ref = rest[-1]
    same = (iota((TILE, TILE), 0) >> HEAD_SHIFT) == (iota((TILE, TILE), 1) >> HEAD_SHIFT)
    mean = jnp.where(same, 1.0 / HEAD_DIM, 0.0).astype(bf16)
    for t in range(out_ref.shape[1] // TILE):
        cols = slice(t * TILE, (t + 1) * TILE)
        here = pl.ds(pl.multiple_of(pl.program_id(0) * out_ref.shape[1] + t * TILE, TILE), TILE)
        entering = jnp.concatenate([mine_ref[:, here], other_ref[:, here]], axis=0)
        gain = gain_ref[:, cols]
        for s in range(NSUB):
            rows = slice(s * SUB, (s + 1) * SUB)
            carried = dot(c_ref[rows, :], entering)
            gated = p_ref[rows, here].astype(f32) + carried * g_ref[rows, here].astype(f32)
            meansq = dot((gated * gated).astype(bf16), mean)
            out_ref[rows, cols] = (gated * lax.rsqrt(meansq + 1e-05) * gain).astype(bf16)


def full(shape):
    return pl.BlockSpec(shape, lambda *i: (0,) * len(shape))


def call(kernel, operands, in_specs, after=(), limit=16, cost=1, **kwargs):
    count = len(operands)

    def ordered(*refs):
        kernel(*refs[:count], *refs[count + len(after) :])

    return pl.pallas_call(
        ordered,
        in_specs=list(in_specs) + [pl.BlockSpec(memory_space=pl.ANY)] * len(after),
        compiler_params=pltpu.CompilerParams(vmem_limit_bytes=limit * MIB),
        cost_estimate=pl.CostEstimate(flops=1, bytes_accessed=cost, transcendentals=0),
        **kwargs,
    )(*operands, *after)


def per_device(
    features,
    output_switch,
    input_proj,
    output_proj,
    step_codes,
    head_rate,
    conv_weight,
    conv_bias,
    bypass_factor,
    norm_gain,
):
    tokens, width = features.shape
    heads = head_rate.shape[0]
    groups = input_proj.shape[1] // NSTATE
    assert tokens == BLOCK and width == heads * HEAD_DIM
    runs = lax.axis_size("ctx")
    pairs = runs // 2
    swap = [(i, i ^ 1) for i in range(runs)]

    def shape(dims, dtype):
        return jax.ShapeDtypeStruct(dims, dtype)

    group_width = width // groups
    per_group = heads // groups
    half = NSTATE // 2
    assert sum(WIDTHS) == width
    hbm = pl.BlockSpec(memory_space=pltpu.HBM)

    def last_rows_kernel(x_ref, out_ref):
        out_ref[...] = x_ref[...].astype(f32)[16 - TAIL :].astype(bf16)

    last_rows = call(
        last_rows_kernel,
        (features,),
        [pl.BlockSpec((16, width), lambda i: (tokens // 16 - 1, 0))],
        limit=16,
        cost=TAIL_BYTES,
        grid=(1,),
        out_specs=full((TAIL, width)),
        out_shape=shape((TAIL, width), bf16),
    )
    tail = lax.ppermute(last_rows, "ctx", [(i, i + 1) for i in range(runs - 1)])
    prepared = (
        ((tokens, 4 * heads), bf16),
        ((4 * per_group, group_width), bf16),
        ((groups * NSTATE, tokens), bf16),
        ((16, width), f32),
        ((8, width), f32),
        ((1, width), f32),
        ((1, width), f32),
    )
    pieces, spread, bt, rows, taps, decay, parity = call(
        prep_kernel,
        (
            step_codes.T, head_rate[None], bypass_factor[None], input_proj, conv_weight,
            conv_bias.reshape(width // 128, 128),
        ),
        [hbm] * 6,
        after=(last_rows,),
        limit=PREP_LIMIT,
        cost=PREP_BYTES,
        grid=(1,),
        out_specs=[full(dims) for dims, _ in prepared],
        out_shape=[shape(*kind) for kind in prepared],
        scratch_shapes=[
            pltpu.VMEM((heads, tokens), jnp.int32),
            pltpu.VMEM((1, heads), f32),
            pltpu.VMEM((1, heads), f32),
            pltpu.VMEM((tokens, groups * NSTATE), bf16),
            pltpu.VMEM((KERNEL, width), bf16),
            pltpu.VMEM((width // 128, 128), bf16),
            pltpu.SemaphoreType.DMA((6,)),
        ],
    )

    def mixing_parts(decay, after):
        kinds = (
            ((tokens, 16 * heads), bf16),
            ((16 * heads, tokens), bf16),
            ((groups, tokens, SUB), f32),
            ((tokens, groups * NSTATE), bf16),
            ((1, width), f32),
        )
        return call(
            mixing_kernel,
            (decay, pieces, bt, output_proj),
            [full((1, width)), full((tokens, 4 * heads)), full((groups * NSTATE, tokens)), full((tokens, groups * NSTATE))],
            after,
            grid=(1,),
            out_specs=[full(dims) for dims, _ in kinds],
            out_shape=[shape(*kind) for kind in kinds],
        )

    gain = norm_gain[None]
    vmem = pl.BlockSpec(memory_space=pltpu.VMEM)

    def conv_states(start, lanes, decay, after):
        return call(
            functools.partial(state_kernel, start),
            (decay, features, tail, taps, pieces, spread, bt, rows),
            [vmem] * 8,
            after,
            limit=STATE_LIMIT,
            cost=STATE_BYTES,
            out_specs=[vmem] * 5,
            out_shape=(
                shape((tokens, lanes), bf16),
                shape((NSUB - 1, NSTATE, lanes), bf16),
                shape((half, lanes), bf16),
                shape((half, lanes), bf16),
                shape((1, width), f32),
            ),
        )

    def inside(start, lanes, inner, whole, filtered, local, filled, decay, after):
        heads_here = ILANES // HEAD_DIM
        return call(
            functools.partial(inside_kernel, start, inner, lanes),
            (decay, output_switch, filtered, local, reads, pieces, spread, left, right, scores, rows, head_rate, *filled),
            [vmem] * 11 + [pl.BlockSpec(memory_space=pltpu.SMEM)] + [vmem] * len(filled),
            after,
            limit=INSIDE_LIMIT,
            cost=INSIDE_BYTES,
            out_specs=[vmem] * 3,
            out_shape=(shape((1, width), f32), shape((tokens, whole), bf16), shape((tokens, whole), bf16)),
            input_output_aliases={12: 1, 13: 2} if filled else {},
            scratch_shapes=[pltpu.VMEM((16 * heads_here, heads_here * SUB), bf16)],
        )

    def final(start, lanes, inner, out, kept, growth, own, other, after):
        block = FLANES if start % FLANES == 0 and lanes % FLANES == 0 else LANES
        first = start // block
        column = lambda i: (0, first + i)
        operands = [kept, growth, own, other, reads, gain]
        in_specs = [
            vmem,
            vmem,
            vmem,
            vmem,
            pl.BlockSpec((tokens, NSTATE), lambda i: (0, (first + i) * block // group_width)),
            pl.BlockSpec((1, block), column),
        ]
        aliases = {}
        if out is not None:
            aliases = {len(operands): 0}
            operands.append(out)
            in_specs.append(pl.BlockSpec(memory_space=pl.ANY))
        return call(
            final_kernel,
            operands,
            in_specs,
            after,
            limit=FINAL_LIMIT,
            cost=FINAL_BYTES,
            grid=(lanes // block,),
            out_specs=pl.BlockSpec((tokens, block), column),
            out_shape=shape((tokens, width), bf16),
            input_output_aliases=aliases,
        )

    def carry(c, own, given):
        cols = slice(starts[c], starts[c] + WIDTHS[c])
        got = lax.ppermute(given, "ctx", swap)
        yield given

        odd = parity[:, cols] > 0.5

        def coefficients():
            mine, theirs = now["decay"][:, cols], now["other"][:, cols]
            return jnp.where(odd, theirs, mine), jnp.where(odd, mine, theirs)

        own, got = own.astype(f32), got.astype(f32)
        before, behind = jnp.where(odd, got, own), jnp.where(odd, own, got)
        entering = None
        for step in range(pairs - 1):
            even, later = coefficients()
            sent = before if entering is None else even * entering + before
            sent = (later * sent + behind).astype(bf16)
            route = [(2 * step + k, 2 * step + 2 + k) for k in range(2)]
            arrived = lax.ppermute(sent, "ctx", route).astype(f32)
            yield sent
            entering = arrived if entering is None else entering + arrived
        even, later = coefficients()
        between = before if entering is None else even * entering + before
        entering = jnp.zeros_like(between) if entering is None else entering
        mine = jnp.where(odd, between, entering).astype(bf16)
        given = jnp.where(odd, entering, between).astype(bf16)
        other = lax.ppermute(given, "ctx", swap)
        yield given
        yield mine, other

    starts = [sum(WIDTHS[:c]) for c in range(len(WIDTHS))]
    now = {"decay": decay}
    travel, entering, remaining = [], {}, []

    def advance(*chosen):
        waited = []
        for c, steps in enumerate(travel):
            if remaining[c] and c in (chosen or range(len(WIDTHS))):
                value = next(steps)
                remaining[c] -= 1
                if remaining[c]:
                    waited.append(value)
                else:
                    entering[c] = value
        return tuple(waited)

    def splits(lanes):
        return [(k, min(IWIDTH, lanes - k)) for k in range(0, lanes, IWIDTH)]

    made, token = [], ()
    for c, lanes in enumerate(WIDTHS):
        made.append(conv_states(starts[c], lanes, now["decay"], token))
        now["decay"] = made[c][4]
        if c == 0:
            now["other"] = lax.ppermute(now["decay"], "ctx", swap)
        travel.append(carry(c, made[c][2], made[c][3]))
        remaining.append(pairs + 2)
        token = advance(c)
    left, right, scores, reads, now["decay"] = mixing_parts(now["decay"], token)
    token = advance(*range(len(WIDTHS) - 1))
    calls = [(c, inner, size) for c, lanes in enumerate(WIDTHS) for inner, size in splits(lanes)]
    kept = [() for _ in WIDTHS]
    for k, (c, inner, size) in enumerate(calls):
        now["decay"], *kept[c] = inside(
            starts[c] + inner, size, inner, WIDTHS[c], made[c][0], made[c][1], kept[c], now["decay"], token
        )
        token = advance()
    out = None
    for c, lanes in enumerate(WIDTHS):
        while c not in entering:
            token = advance()
        out = final(starts[c], lanes, 0, out, *kept[c], *entering[c], token)
        token = advance()
    return out


def solution(mesh):
    placed = (
        P(("groups", "ctx"), "head"),
        P(("groups", "ctx"), "head"),
        P(("groups", "ctx"), "head"),
        P(("groups", "ctx"), "head"),
        P(("groups", "ctx"), "head"),
        P("head"),
        P(None, "head"),
        P("head"),
        P("head"),
        P("head"),
    )
    return jax.shard_map(
        per_device,
        mesh=mesh,
        in_specs=placed,
        out_specs=P(("groups", "ctx"), "head"),
        check_vma=False,
    )
```
